32 devices in a mesh: dp: 4 (over x, core), tensor: 8 (over z, y).
Axes of the slice: x: 2, y: 2, z: 4, core: 2. Of those that a mesh axis runs over, the one named last changes fastest.
Arguments:
- hidden: bfloat16 [1024, 8192], P('dp', 'tensor'), may hold values from -170 to 170, as said below
- neighbour_ids: int32 [16, 2], P('dp'), may hold values from 0 to 127, as said below
- database: bfloat16 [128, 128, 8192], P('dp', None, 'tensor'), may hold values from -6 to 6
- w_query: bfloat16 [8192, 4096], P(None, 'tensor'), may hold values from -0.0625 to 0.0625
- w_key: bfloat16 [8192, 4096], P(None, 'tensor'), may hold values from -0.0625 to 0.0625
- w_value: bfloat16 [8192, 4096], P(None, 'tensor'), may hold values from -0.0625 to 0.0625
- w_out: bfloat16 [4096, 8192], P('tensor'), may hold values from -0.09375 to 0.09375
Outputs:
- mixed: bfloat16 [1024, 8192], P('dp', 'tensor')
The draws below stay inside these ranges and needn't reach their ends.
Inputs may be any that keep to these rules, and one draw needn't show every extreme that they name: `neighbour_ids`: database block b is held by index b // 32 of dp. Among the 8 neighbour ids of one sequence (the rows of one device), at most 4 belong to the same holder, and in every sequence exactly 4 do. `hidden`: hidden states may be large for some tokens.
All inputs are finite; a program needn't handle non-finite values.
Results may differ from the reference program's by a relative error of at most 0.02.
Values may be sent and summed in bfloat16 or wider, within the bound.
A program may use at most 128 MiB of HBM per device.

```python
import jax
import jax.numpy as jnp
from jax import lax

D = 8192
HEADS = 32
HD = 128
GROUP = 64
RET = 128
NEIGH = 2
TOK_DEV = 256
DB_DEV = 32
TOKENS = 1024
BLOCKS = 128
N_DP = 4


def draw_hidden(key, part):
    first_key = jax.random.fold_in(key, 0)
    base_values = jnp.clip(jax.random.normal(first_key, (TOKENS, D), jnp.float32), -6.0, 6.0)
    return base_values.astype(jnp.bfloat16)


def draw_neighbour_ids(key, part):
    keys_list = jax.random.split(key, 5)
    dp_count = TOKENS // TOK_DEV
    per_reader = NEIGH * TOK_DEV // GROUP
    capacity = per_reader // 2
    base_owner = jax.random.randint(keys_list[0], (), 0, dp_count)
    hot_owner = (base_owner + jax.random.randint(keys_list[1], (dp_count,), 0, max(dp_count // 4, 1))) % dp_count
    other_owner = (hot_owner[:, None] + 1 + jax.random.randint(keys_list[2], (dp_count, per_reader - capacity), 0, dp_count - 1)) % dp_count
    owners = jnp.concatenate([jnp.broadcast_to(hot_owner[:, None], (dp_count, capacity)), other_owner], 1)
    order_keys = jax.random.split(keys_list[3], dp_count)
    orders = jax.vmap(lambda order_key: jax.random.permutation(order_key, per_reader))(order_keys)
    owners = jnp.take_along_axis(owners, orders, axis=1)
    local_index = jax.random.randint(keys_list[4], (dp_count, per_reader), 0, DB_DEV)
    block_ids = owners * DB_DEV + local_index
    return block_ids.reshape(TOKENS // GROUP, NEIGH).astype(jnp.int32)


def steps_of(stream_key, shape, cuts, low, largest):
    def one(dim, parts):
        heights = jax.random.uniform(jax.random.fold_in(jax.random.fold_in(stream_key, 6), dim), (parts,), jnp.float32, low / len(cuts), largest / len(cuts))
        return jnp.repeat(jnp.exp(heights), shape[dim] // parts).reshape((-1,) + (1,) * (len(shape) - dim - 1))

    level = one(*cuts[0])
    for cut in cuts[1:]:
        level = level * one(*cut)
    return level


def gaussian(own_key, extent, scale, limit, cuts=(), kind=jnp.bfloat16):
    entries = scale * jax.random.normal(own_key, extent, jnp.float32)
    if cuts:
        entries = entries * steps_of(own_key, extent, cuts, -0.22, 0.18)
    return jnp.clip(entries, -limit, limit).astype(kind)


def setup_inputs(seed: int = 0) -> dict:
    seeds = jax.random.split(jax.random.key(seed), 8)
    return {
        "hidden": draw_hidden(jax.random.fold_in(seeds[7], 71), 0),
        "neighbour_ids": draw_neighbour_ids(jax.random.fold_in(seeds[7], 71), 0),
        "database": gaussian(seeds[2], (BLOCKS, RET, D), 1.0, 6.0, ((0, 4), (2, 8))),
        "w_query": gaussian(seeds[3], (D, HEADS * HD), D ** -0.5, 0.0625, ((1, 8),)),
        "w_key": gaussian(seeds[4], (D, HEADS * HD), D ** -0.5, 0.0625, ((1, 8),)),
        "w_value": gaussian(seeds[5], (D, HEADS * HD), D ** -0.5, 0.0625, ((1, 8),)),
        "w_out": gaussian(seeds[6], (HEADS * HD, D), (HEADS * HD) ** -0.5, 0.09375, ((0, 8),)),
    }


def attend(query_rows, key_rows, value_rows, heads_count, group_len):
    tok_count, width = query_rows.shape
    groups = tok_count // group_len
    head_size = width // heads_count
    shifted = jnp.concatenate([query_rows[group_len - 1:], jnp.zeros((group_len - 1, width), jnp.bfloat16)], 0)
    shifted = shifted.reshape(groups, group_len, heads_count, head_size).astype(jnp.float32)
    key_block = key_rows.reshape(groups, -1, heads_count, head_size).astype(jnp.float32)
    value_block = value_rows.reshape(groups, -1, heads_count, head_size).astype(jnp.float32)
    scores = jnp.einsum('cqhd,ckhd->chqk', shifted, key_block) / jnp.sqrt(jnp.float32(head_size))
    top_score = lax.optimization_barrier(jnp.max(scores, axis=-1, keepdims=True))
    weights_raw = jnp.exp(scores - top_score)
    soft = (weights_raw / lax.optimization_barrier(jnp.sum(weights_raw, axis=-1, keepdims=True))).astype(jnp.bfloat16)
    blended = jnp.einsum('chqk,ckhd->cqhd', soft.astype(jnp.float32), value_block).astype(jnp.bfloat16)
    blended = blended.reshape(tok_count, width)
    return jnp.concatenate([jnp.zeros((group_len - 1, width), jnp.bfloat16), blended[:tok_count - group_len + 1]], 0)

def reference(hidden, neighbour_ids, database, w_query, w_key, w_value, w_out):
    query_rows = jnp.dot(hidden, w_query, preferred_element_type=jnp.float32).astype(jnp.bfloat16)
    shard_query = query_rows.reshape(N_DP, TOK_DEV, HEADS * HD)
    shard_ids = neighbour_ids.reshape(N_DP, NEIGH * TOK_DEV // GROUP)

    def one_shard(pair):
        query_part, id_part = pair
        gathered = jnp.take(database, id_part, axis=0).reshape(-1, D)
        key_rows = jnp.dot(gathered, w_key, preferred_element_type=jnp.float32).astype(jnp.bfloat16)
        value_rows = jnp.dot(gathered, w_value, preferred_element_type=jnp.float32).astype(jnp.bfloat16)
        return attend(query_part, key_rows, value_rows, HEADS, GROUP)
    contexts = lax.map(one_shard, (shard_query, shard_ids)).reshape(TOKENS, HEADS * HD)
    return jnp.dot(contexts, w_out, preferred_element_type=jnp.float32).astype(jnp.bfloat16)
```

```python
import functools

import jax
import jax.numpy as jnp
from jax import lax
from jax.experimental import pallas as pl
from jax.experimental.pallas import tpu as pltpu
from jax.sharding import PartitionSpec as P

MESH = pl.DeviceIdType.MESH

HD = 128


def attend(query_rows, key_rows, value_rows, heads_count, group_len):
    tok_count, width = query_rows.shape
    groups = tok_count // group_len
    head_size = width // heads_count
    shifted = jnp.concatenate(
        [query_rows[group_len - 1 :], jnp.zeros((group_len - 1, width), jnp.bfloat16)], 0
    )
    shifted = shifted.reshape(groups, group_len, heads_count, head_size)
    key_block = key_rows.reshape(groups, -1, heads_count, head_size)
    value_block = value_rows.reshape(groups, -1, heads_count, head_size)
    scores = jnp.einsum(
        "cqhd,ckhd->chqk", shifted, key_block, preferred_element_type=jnp.float32
    ) / jnp.sqrt(jnp.float32(head_size))
    top_score = jnp.max(scores, axis=-1, keepdims=True)
    weights_raw = jnp.exp(scores - top_score)
    soft = (weights_raw / jnp.sum(weights_raw, axis=-1, keepdims=True)).astype(jnp.bfloat16)
    blended = jnp.einsum(
        "chqk,ckhd->cqhd", soft, value_block, preferred_element_type=jnp.float32
    ).astype(jnp.bfloat16)
    blended = blended.reshape(tok_count, width)
    return jnp.concatenate(
        [jnp.zeros((group_len - 1, width), jnp.bfloat16), blended[: tok_count - group_len + 1]], 0
    )


def plane(tensor_count):
    nz = 4 if tensor_count % 4 == 0 else 1
    return nz, tensor_count // nz


def gather_project(
    nz, ny, x_ref, wk_ref, wv_ref, k_ref, v_ref,
    held, wk_held, wv_held, total, send_sem, recv_sem, local_sem,
):
    chunks, rows, feats = x_ref.shape
    cols = wk_ref.shape[1]
    me = lax.axis_index("tensor")
    z, y = me // ny, me % ny
    up, down, right, left = z + 1 < nz, z >= 1, y + 1 < ny, y >= 1

    own_copy = pltpu.make_async_copy(x_ref, held.at[me], local_sem.at[0])
    own_copy.start()
    wk_copy = pltpu.make_async_copy(wk_ref, wk_held, local_sem.at[1])
    wk_copy.start()
    wv_copy = pltpu.make_async_copy(wv_ref, wv_held, local_sem.at[2])
    wv_copy.start()

    barrier = pltpu.get_barrier_semaphore()
    sides = ((up, ny), (down, -ny), (right, 1), (left, -1))
    for there, step in sides:
        @pl.when(there)
        def _():
            pl.semaphore_signal(
                barrier, inc=1, device_id={"tensor": me + step}, device_id_type=MESH
            )
    pl.semaphore_wait(barrier, sum(there.astype(jnp.int32) for there, _ in sides))

    def move(side, shard, c):
        return pltpu.make_async_remote_copy(
            src_ref=held.at[shard, c],
            dst_ref=held.at[shard, c],
            send_sem=send_sem.at[side, shard, c],
            recv_sem=recv_sem.at[shard, c],
            device_id={"tensor": me + sides[side][1]},
            device_id_type=MESH,
        )

    def send(side, shard, c, cond):
        @pl.when(cond & sides[side][0])
        def _():
            move(side, shard, c).start()

    def landed(shard, c):
        move(0, shard, c).wait_recv()

    total[...] = jnp.zeros_like(total)
    own_copy.wait()

    def column(e):
        step = (e + 1) // 2
        above = e % 2 == 0
        zc = jnp.where(above, z + step, z - step)
        return zc, above, step, (zc >= 0) & (zc < nz) & (e >= 0) & (e < 2 * nz - 1)

    def project(shard):
        w_rows = pl.ds(pl.multiple_of(shard * feats, feats), feats)

        @pl.loop(0, chunks)
        def _(c):
            block = held[shard, c]
            total[c, :, :cols] += jnp.dot(
                block, wk_held[w_rows, :], preferred_element_type=jnp.float32
            )
            total[c, :, cols:] += jnp.dot(
                block, wv_held[w_rows, :], preferred_element_type=jnp.float32
            )

    def event(e, carry):
        zc, above, step, valid = column(e)

        @pl.when(valid)
        def _():
            shard = zc * ny + y
            for c in range(chunks):
                @pl.when(step > 0)
                def _():
                    landed(shard, c)

                send(0, shard, c, (step == 0) | jnp.logical_not(above))
                send(1, shard, c, above)
                send(2, shard, c, True)
                send(3, shard, c, True)

            @pl.when(step == 0)
            def _():
                wk_copy.wait()
                wv_copy.wait()

            project(shard)

        zl, _, _, late = column(e - 2)
        for m in range(1, ny):
            for sign in (-1, 1):
                yc = y + sign * m

                @pl.when(late & (yc >= 0) & (yc < ny))
                def _():
                    shard = zl * ny + yc
                    for c in range(chunks):
                        landed(shard, c)
                        if ny > 2:
                            send(2 if sign < 0 else 3, shard, c, True)
                    project(shard)
        return carry

    lax.fori_loop(0, 2 * nz + 1, event, 0)

    k_ref[...] = total[:, :, :cols].astype(jnp.bfloat16)
    v_ref[...] = total[:, :, cols:].astype(jnp.bfloat16)

    def finish(shard, carry):
        zs, ys = shard // ny, shard % ny
        mine = ys == y
        went = (mine & (zs <= z), mine & (zs >= z), ys <= y, ys >= y)
        for side in range(4):
            @pl.when(went[side] & sides[side][0])
            def _():
                for c in range(chunks):
                    move(side, shard, c).wait_send()
        return carry

    lax.fori_loop(0, nz * ny, finish, 0)


def neighbour_keys(rows, w_key, w_value, chunks):
    tensor_count = lax.axis_size("tensor")
    nz, ny = plane(tensor_count)
    row_count, feats = rows.shape
    cols = w_key.shape[1]
    per = row_count // chunks
    out = jax.ShapeDtypeStruct((chunks, per, cols), jnp.bfloat16)
    keys, values = pl.pallas_call(
        functools.partial(gather_project, nz, ny),
        out_shape=(out, out),
        in_specs=[pl.BlockSpec(memory_space=pl.ANY)] * 3,
        out_specs=(pl.BlockSpec(memory_space=pltpu.VMEM),) * 2,
        scratch_shapes=[
            pltpu.VMEM((tensor_count, chunks, per, feats), jnp.bfloat16),
            pltpu.VMEM(w_key.shape, jnp.bfloat16),
            pltpu.VMEM(w_value.shape, jnp.bfloat16),
            pltpu.VMEM((chunks, per, 2 * cols), jnp.float32),
            pltpu.SemaphoreType.DMA((4, tensor_count, chunks)),
            pltpu.SemaphoreType.DMA((tensor_count, chunks)),
            pltpu.SemaphoreType.DMA((3,)),
        ],
        compiler_params=pltpu.CompilerParams(
            collective_id=0, has_side_effects=True, vmem_limit_bytes=56 * 2**20
        ),
        cost_estimate=pl.CostEstimate(
            flops=4 * row_count * feats * tensor_count * cols,
            bytes_accessed=4 * w_key.size,
            transcendentals=0,
        ),
    )(rows.reshape(chunks, per, feats), w_key, w_value)
    return keys.reshape(row_count, cols), values.reshape(row_count, cols)


def project_scatter(
    nz, ny, ctx_ref, w_ref, out_ref, w_held, outgoing, from_y, from_z,
    total, send_sem, recv_y, recv_z, local_sem,
):
    feats = out_ref.shape[1]
    count = nz * ny
    me = lax.axis_index("tensor")
    z, y = me // ny, me % ny
    up, down, right, left = z + 1 < nz, z >= 1, y + 1 < ny, y >= 1
    sides = ((up, ny), (down, -ny), (right, 1), (left, -1))

    def load(dest):
        columns = pl.ds(pl.multiple_of(dest * feats, feats), feats)
        return pltpu.make_async_copy(
            w_ref.at[:, columns], w_held.at[dest], local_sem.at[dest]
        )

    def column(e):
        step = (e + 1) // 2
        above = e % 2 == 0
        zc = jnp.where(above, z + step, z - step)
        return zc, above, (zc >= 0) & (zc < nz) & (e >= 0) & (e < 2 * nz - 1)

    def fetch(i, carry):
        zc, _, valid = column(2 * nz - 2 - i)

        @pl.when(valid)
        def _():
            for off in range(1, ny + 1):
                load(zc * ny + (y + off) % ny).start()
        return carry

    lax.fori_loop(0, 2 * nz - 1, fetch, 0)

    barrier = pltpu.get_barrier_semaphore()
    for there, step in sides:
        @pl.when(there)
        def _():
            pl.semaphore_signal(
                barrier, inc=1, device_id={"tensor": me + step}, device_id_type=MESH
            )
    pl.semaphore_wait(barrier, sum(there.astype(jnp.int32) for there, _ in sides))

    def along_y(side, dest):
        return pltpu.make_async_remote_copy(
            src_ref=outgoing.at[dest],
            dst_ref=from_y.at[side, dest],
            send_sem=send_sem.at[dest],
            recv_sem=recv_y.at[side, dest],
            device_id={"tensor": me + (1 if side == 0 else -1)},
            device_id_type=MESH,
        )

    def along_z(side, dest):
        return pltpu.make_async_remote_copy(
            src_ref=outgoing.at[dest],
            dst_ref=from_z.at[side, dest // ny],
            send_sem=send_sem.at[dest],
            recv_sem=recv_z.at[side, dest // ny],
            device_id={"tensor": me + (ny if side == 0 else -ny)},
            device_id_type=MESH,
        )

    def own_share(dest):
        load(dest).wait()
        return jnp.dot(ctx_ref[...], w_held[dest], preferred_element_type=jnp.float32)

    def event(i, carry):
        zc, _, valid = column(2 * nz - 2 - i)
        for m in range(ny - 1, 0, -1):
            for side in (0, 1):
                yc = y + m if side == 0 else y - m

                @pl.when(valid & (yc >= 0) & (yc < ny))
                def _():
                    dest = zc * ny + yc
                    share = own_share(dest)
                    outgoing[dest] = share.astype(jnp.bfloat16)
                    if ny > 2:
                        @pl.when(left if side == 0 else right)
                        def _():
                            along_y(side, dest).wait_recv()
                            outgoing[dest] = (
                                share + from_y[side, dest].astype(jnp.float32)
                            ).astype(jnp.bfloat16)
                    along_y(side, dest).start()

        zl, above, late = column(2 * nz - 2 - i + 2)

        @pl.when(late)
        def _():
            dest = zl * ny + y
            share = own_share(dest)
            total[...] = share
            for side, there in ((0, left), (1, right)):
                @pl.when(there)
                def _():
                    along_y(side, dest).wait_recv()
                    total[...] += from_y[side, dest].astype(jnp.float32)
            for side, there in ((0, down & (zl >= z)), (1, up & (zl <= z))):
                @pl.when(there)
                def _():
                    along_z(side, dest).wait_recv()
                    total[...] += from_z[side, zl].astype(jnp.float32)

            @pl.when(zl == z)
            def _():
                out_ref[...] = total[...].astype(jnp.bfloat16)

            @pl.when(zl != z)
            def _():
                outgoing[dest] = total[...].astype(jnp.bfloat16)

            @pl.when(zl > z)
            def _():
                along_z(0, dest).start()

            @pl.when(zl < z)
            def _():
                along_z(1, dest).start()
        return carry

    lax.fori_loop(0, 2 * nz + 1, event, 0)

    def finish(dest, carry):
        @pl.when(dest != me)
        def _():
            along_y(0, dest).wait_send()
        return carry

    lax.fori_loop(0, count, finish, 0)


def project_out(context, w_out):
    tensor_count = lax.axis_size("tensor")
    nz, ny = plane(tensor_count)
    rows, depth = context.shape
    feats = w_out.shape[1] // tensor_count
    return pl.pallas_call(
        functools.partial(project_scatter, nz, ny),
        out_shape=jax.ShapeDtypeStruct((rows, feats), jnp.bfloat16),
        in_specs=[
            pl.BlockSpec(memory_space=pltpu.VMEM),
            pl.BlockSpec(memory_space=pl.ANY),
        ],
        out_specs=pl.BlockSpec(memory_space=pltpu.VMEM),
        scratch_shapes=[
            pltpu.VMEM((tensor_count, depth, feats), jnp.bfloat16),
            pltpu.VMEM((tensor_count, rows, feats), jnp.bfloat16),
            pltpu.VMEM((2, tensor_count, rows, feats), jnp.bfloat16),
            pltpu.VMEM((2, nz, rows, feats), jnp.bfloat16),
            pltpu.VMEM((rows, feats), jnp.float32),
            pltpu.SemaphoreType.DMA((tensor_count,)),
            pltpu.SemaphoreType.DMA((2, tensor_count)),
            pltpu.SemaphoreType.DMA((2, nz)),
            pltpu.SemaphoreType.DMA((tensor_count,)),
        ],
        compiler_params=pltpu.CompilerParams(
            collective_id=1, has_side_effects=True, vmem_limit_bytes=48 * 2**20
        ),
        cost_estimate=pl.CostEstimate(
            flops=2 * rows * w_out.size, bytes_accessed=2 * w_out.size, transcendentals=0
        ),
    )(context, w_out)


def shards(hidden, neighbour_ids, database, w_query, w_key, w_value, w_out):
    dp_count = lax.axis_size("dp")
    tok_rows = hidden.shape[0]
    group_count = neighbour_ids.shape[0]
    per_reader = group_count * neighbour_ids.shape[1]
    capacity = per_reader // 2
    db_count = database.shape[0]
    ret_len = database.shape[1]
    col_count = database.shape[2]
    head_cols = w_query.shape[1]
    heads_local = head_cols // HD
    query_sum = jnp.dot(
        lax.all_gather(hidden, "tensor", axis=1, tiled=True),
        w_query,
        preferred_element_type=jnp.float32,
    )
    query_rows = query_sum.astype(jnp.bfloat16)
    block_ids = neighbour_ids.reshape(per_reader)
    owners = block_ids // db_count
    earlier = jnp.arange(per_reader)[:, None] > jnp.arange(per_reader)[None, :]
    slot_rank = jnp.sum(((owners[:, None] == owners[None, :]) & earlier).astype(jnp.int32), 1)
    slot_range = jnp.arange(capacity, dtype=jnp.int32)
    local_index = block_ids % db_count
    owner_range = jnp.arange(dp_count, dtype=jnp.int32)
    slot_hit = (owners[:, None, None] == owner_range[None, :, None]) & (
        slot_rank[:, None, None] == slot_range[None, None, :]
    )
    request_table = jnp.sum(slot_hit.astype(jnp.int32) * local_index[:, None, None], 0)
    requested = lax.all_to_all(request_table, "dp", split_axis=0, concat_axis=0, tiled=True)
    outgoing = jnp.take(database, requested.reshape(-1), axis=0).reshape(
        dp_count, capacity, ret_len, col_count
    )
    arrived = lax.all_to_all(outgoing, "dp", split_axis=0, concat_axis=0, tiled=True)
    neighbour_rows = jnp.take(
        arrived.reshape(dp_count * capacity, ret_len, col_count),
        owners * capacity + slot_rank,
        axis=0,
    )
    key_rows, value_rows = neighbour_keys(
        neighbour_rows.reshape(per_reader * ret_len, col_count), w_key, w_value, group_count
    )
    context = attend(query_rows, key_rows, value_rows, heads_local, tok_rows // group_count)
    skipped = (tok_rows // group_count - 1) // 16 * 16
    mixed = project_out(context[skipped:], w_out)
    return jnp.concatenate([jnp.zeros((skipped, mixed.shape[1]), mixed.dtype), mixed], 0)


def solution(mesh):
    placed = (
        P("dp", "tensor"),
        P("dp", None),
        P("dp", None, "tensor"),
        P(None, "tensor"),
        P(None, "tensor"),
        P(None, "tensor"),
        P("tensor", None),
    )
    return jax.shard_map(
        shards, mesh=mesh, in_specs=placed, out_specs=P("dp", "tensor"), check_vma=False
    )
```

```python
import functools

import jax
import jax.numpy as jnp
from jax import lax
from jax.experimental import pallas as pl
from jax.experimental.pallas import tpu as pltpu
from jax.sharding import PartitionSpec as P

MESH = pl.DeviceIdType.MESH

HD = 128


def attend(query_rows, key_rows, value_rows, heads_count, group_len):
    width = query_rows.shape[1]
    groups = query_rows.shape[0] // group_len
    head_size = width // heads_count
    shifted = query_rows.reshape(groups, group_len, heads_count, head_size)
    key_block = key_rows.reshape(groups, -1, heads_count, head_size)
    value_block = value_rows.reshape(groups, -1, heads_count, head_size)
    scores = jnp.einsum(
        "cqhd,ckhd->chqk", shifted, key_block, preferred_element_type=jnp.float32
    ) / jnp.sqrt(jnp.float32(head_size))
    soft = softmax(scores)
    blended = jnp.einsum(
        "chqk,ckhd->cqhd", soft, value_block, preferred_element_type=jnp.float32
    ).astype(jnp.bfloat16)
    return blended.reshape(groups * group_len, width)


def softmax(scores):
    top_score = jnp.max(scores, axis=-1, keepdims=True)
    weights_raw = jnp.exp(scores - top_score)
    return (weights_raw / jnp.sum(weights_raw, axis=-1, keepdims=True)).astype(jnp.bfloat16)


def plane(tensor_count):
    nz = 4 if tensor_count % 4 == 0 else 1
    return nz, tensor_count // nz


def gather_project(
    nz, ny, x_ref, wk_ref, wv_ref, k_ref, v_ref,
    held, wk_held, wv_held, total, send_sem, recv_sem, local_sem,
):
    chunks, rows, feats = x_ref.shape
    cols = wk_ref.shape[1]
    me = lax.axis_index("tensor")
    z, y = me // ny, me % ny
    up, down, right, left = z + 1 < nz, z >= 1, y + 1 < ny, y >= 1

    own_copy = pltpu.make_async_copy(x_ref, held.at[me], local_sem.at[0])
    own_copy.start()
    wk_copy = pltpu.make_async_copy(wk_ref, wk_held, local_sem.at[1])
    wk_copy.start()
    wv_copy = pltpu.make_async_copy(wv_ref, wv_held, local_sem.at[2])
    wv_copy.start()

    barrier = pltpu.get_barrier_semaphore()
    sides = ((up, ny), (down, -ny), (right, 1), (left, -1))
    for there, step in sides:
        @pl.when(there)
        def _():
            pl.semaphore_signal(
                barrier, inc=1, device_id={"tensor": me + step}, device_id_type=MESH
            )
    pl.semaphore_wait(barrier, sum(there.astype(jnp.int32) for there, _ in sides))

    def move(side, shard, c):
        return pltpu.make_async_remote_copy(
            src_ref=held.at[shard, c],
            dst_ref=held.at[shard, c],
            send_sem=send_sem.at[side, shard, c],
            recv_sem=recv_sem.at[shard, c],
            device_id={"tensor": me + sides[side][1]},
            device_id_type=MESH,
        )

    def send(side, shard, c, cond):
        @pl.when(cond & sides[side][0])
        def _():
            move(side, shard, c).start()

    def landed(shard, c):
        move(0, shard, c).wait_recv()

    total[...] = jnp.zeros_like(total)
    own_copy.wait()

    def column(e):
        step = (e + 1) // 2
        above = e % 2 == 0
        zc = jnp.where(above, z + step, z - step)
        return zc, above, step, (zc >= 0) & (zc < nz) & (e >= 0) & (e < 2 * nz - 1)

    def project(shard):
        w_rows = pl.ds(pl.multiple_of(shard * feats, feats), feats)

        @pl.loop(0, chunks)
        def _(c):
            block = held[shard, c]
            total[c, :, :cols] += jnp.dot(
                block, wk_held[w_rows, :], preferred_element_type=jnp.float32
            )
            total[c, :, cols:] += jnp.dot(
                block, wv_held[w_rows, :], preferred_element_type=jnp.float32
            )

    def event(e, carry):
        zc, above, step, valid = column(e)

        @pl.when(valid)
        def _():
            shard = zc * ny + y
            for c in range(chunks):
                @pl.when(step > 0)
                def _():
                    landed(shard, c)

                send(0, shard, c, (step == 0) | jnp.logical_not(above))
                send(1, shard, c, above)
                send(2, shard, c, True)
                send(3, shard, c, True)

            @pl.when(step == 0)
            def _():
                wk_copy.wait()
                wv_copy.wait()

            project(shard)

        zl, _, _, late = column(e - 2)
        for m in range(1, ny):
            for sign in (-1, 1):
                yc = y + sign * m

                @pl.when(late & (yc >= 0) & (yc < ny))
                def _():
                    shard = zl * ny + yc
                    for c in range(chunks):
                        landed(shard, c)
                        if ny > 2:
                            send(2 if sign < 0 else 3, shard, c, True)
                    project(shard)
        return carry

    lax.fori_loop(0, 2 * nz + 1, event, 0)

    k_ref[...] = total[:, :, :cols].astype(jnp.bfloat16)
    v_ref[...] = total[:, :, cols:].astype(jnp.bfloat16)

    def finish(shard, carry):
        zs, ys = shard // ny, shard % ny
        mine = ys == y
        went = (mine & (zs <= z), mine & (zs >= z), ys <= y, ys >= y)
        for side in range(4):
            @pl.when(went[side] & sides[side][0])
            def _():
                for c in range(chunks):
                    move(side, shard, c).wait_send()
        return carry

    lax.fori_loop(0, nz * ny, finish, 0)


def neighbour_keys(rows, w_key, w_value, chunks):
    tensor_count = lax.axis_size("tensor")
    nz, ny = plane(tensor_count)
    row_count, feats = rows.shape
    cols = w_key.shape[1]
    per = row_count // chunks
    out = jax.ShapeDtypeStruct((chunks, per, cols), jnp.bfloat16)
    keys, values = pl.pallas_call(
        functools.partial(gather_project, nz, ny),
        out_shape=(out, out),
        in_specs=[pl.BlockSpec(memory_space=pl.ANY)] * 3,
        out_specs=(pl.BlockSpec(memory_space=pltpu.VMEM),) * 2,
        scratch_shapes=[
            pltpu.VMEM((tensor_count, chunks, per, feats), jnp.bfloat16),
            pltpu.VMEM(w_key.shape, jnp.bfloat16),
            pltpu.VMEM(w_value.shape, jnp.bfloat16),
            pltpu.VMEM((chunks, per, 2 * cols), jnp.float32),
            pltpu.SemaphoreType.DMA((4, tensor_count, chunks)),
            pltpu.SemaphoreType.DMA((tensor_count, chunks)),
            pltpu.SemaphoreType.DMA((3,)),
        ],
        compiler_params=pltpu.CompilerParams(
            collective_id=0, has_side_effects=True, vmem_limit_bytes=56 * 2**20
        ),
        cost_estimate=pl.CostEstimate(
            flops=4 * row_count * feats * tensor_count * cols,
            bytes_accessed=4 * w_key.size,
            transcendentals=0,
        ),
    )(rows.reshape(chunks, per, feats), w_key, w_value)
    return keys.reshape(row_count, cols), values.reshape(row_count, cols)


def project_scatter(
    nz, ny, ctx_ref, w_ref, out_ref, w_held, outgoing, from_y, from_z,
    total, send_sem, recv_y, recv_z, local_sem,
):
    feats = out_ref.shape[1]
    count = nz * ny
    me = lax.axis_index("tensor")
    z, y = me // ny, me % ny
    up, down, right, left = z + 1 < nz, z >= 1, y + 1 < ny, y >= 1
    sides = ((up, ny), (down, -ny), (right, 1), (left, -1))

    def load(dest):
        columns = pl.ds(pl.multiple_of(dest * feats, feats), feats)
        return pltpu.make_async_copy(
            w_ref.at[:, columns], w_held.at[dest], local_sem.at[dest]
        )

    def column(e):
        step = (e + 1) // 2
        above = e % 2 == 0
        zc = jnp.where(above, z + step, z - step)
        return zc, above, (zc >= 0) & (zc < nz) & (e >= 0) & (e < 2 * nz - 1)

    def fetch(i, carry):
        zc, _, valid = column(2 * nz - 2 - i)

        @pl.when(valid)
        def _():
            for off in range(1, ny + 1):
                load(zc * ny + (y + off) % ny).start()
        return carry

    lax.fori_loop(0, 2 * nz - 1, fetch, 0)

    barrier = pltpu.get_barrier_semaphore()
    for there, step in sides:
        @pl.when(there)
        def _():
            pl.semaphore_signal(
                barrier, inc=1, device_id={"tensor": me + step}, device_id_type=MESH
            )
    pl.semaphore_wait(barrier, sum(there.astype(jnp.int32) for there, _ in sides))

    def along_y(side, dest):
        return pltpu.make_async_remote_copy(
            src_ref=outgoing.at[dest],
            dst_ref=from_y.at[side, dest],
            send_sem=send_sem.at[dest],
            recv_sem=recv_y.at[side, dest],
            device_id={"tensor": me + (1 if side == 0 else -1)},
            device_id_type=MESH,
        )

    def along_z(side, dest):
        return pltpu.make_async_remote_copy(
            src_ref=outgoing.at[dest],
            dst_ref=from_z.at[side, dest // ny],
            send_sem=send_sem.at[dest],
            recv_sem=recv_z.at[side, dest // ny],
            device_id={"tensor": me + (ny if side == 0 else -ny)},
            device_id_type=MESH,
        )

    def own_share(dest):
        load(dest).wait()
        return jnp.dot(ctx_ref[...], w_held[dest], preferred_element_type=jnp.float32)

    def event(i, carry):
        zc, _, valid = column(2 * nz - 2 - i)
        for m in range(ny - 1, 0, -1):
            for side in (0, 1):
                yc = y + m if side == 0 else y - m

                @pl.when(valid & (yc >= 0) & (yc < ny))
                def _():
                    dest = zc * ny + yc
                    share = own_share(dest)
                    outgoing[dest] = share.astype(jnp.bfloat16)
                    if ny > 2:
                        @pl.when(left if side == 0 else right)
                        def _():
                            along_y(side, dest).wait_recv()
                            outgoing[dest] = (
                                share + from_y[side, dest].astype(jnp.float32)
                            ).astype(jnp.bfloat16)
                    along_y(side, dest).start()

        zl, above, late = column(2 * nz - 2 - i + 2)

        @pl.when(late)
        def _():
            dest = zl * ny + y
            share = own_share(dest)
            total[...] = share
            for side, there in ((0, left), (1, right)):
                @pl.when(there)
                def _():
                    along_y(side, dest).wait_recv()
                    total[...] += from_y[side, dest].astype(jnp.float32)
            for side, there in ((0, down & (zl >= z)), (1, up & (zl <= z))):
                @pl.when(there)
                def _():
                    along_z(side, dest).wait_recv()
                    total[...] += from_z[side, zl].astype(jnp.float32)

            @pl.when(zl == z)
            def _():
                out_ref[...] = total[...].astype(jnp.bfloat16)

            @pl.when(zl != z)
            def _():
                outgoing[dest] = total[...].astype(jnp.bfloat16)

            @pl.when(zl > z)
            def _():
                along_z(0, dest).start()

            @pl.when(zl < z)
            def _():
                along_z(1, dest).start()
        return carry

    lax.fori_loop(0, 2 * nz + 1, event, 0)

    def finish(dest, carry):
        @pl.when(dest != me)
        def _():
            along_y(0, dest).wait_send()
        return carry

    lax.fori_loop(0, count, finish, 0)


def project_out(context, w_out):
    tensor_count = lax.axis_size("tensor")
    nz, ny = plane(tensor_count)
    rows, depth = context.shape
    feats = w_out.shape[1] // tensor_count
    return pl.pallas_call(
        functools.partial(project_scatter, nz, ny),
        out_shape=jax.ShapeDtypeStruct((rows, feats), jnp.bfloat16),
        in_specs=[
            pl.BlockSpec(memory_space=pltpu.VMEM),
            pl.BlockSpec(memory_space=pl.ANY),
        ],
        out_specs=pl.BlockSpec(memory_space=pltpu.VMEM),
        scratch_shapes=[
            pltpu.VMEM((tensor_count, depth, feats), jnp.bfloat16),
            pltpu.VMEM((tensor_count, rows, feats), jnp.bfloat16),
            pltpu.VMEM((2, tensor_count, rows, feats), jnp.bfloat16),
            pltpu.VMEM((2, nz, rows, feats), jnp.bfloat16),
            pltpu.VMEM((rows, feats), jnp.float32),
            pltpu.SemaphoreType.DMA((tensor_count,)),
            pltpu.SemaphoreType.DMA((2, tensor_count)),
            pltpu.SemaphoreType.DMA((2, nz)),
            pltpu.SemaphoreType.DMA((tensor_count,)),
        ],
        compiler_params=pltpu.CompilerParams(
            collective_id=1, has_side_effects=True, vmem_limit_bytes=48 * 2**20
        ),
        cost_estimate=pl.CostEstimate(
            flops=2 * rows * w_out.size, bytes_accessed=2 * w_out.size, transcendentals=0
        ),
    )(context, w_out)


def shards(hidden, neighbour_ids, database, w_query, w_key, w_value, w_out):
    dp_count = lax.axis_size("dp")
    tok_rows = hidden.shape[0]
    group_count = neighbour_ids.shape[0]
    per_reader = group_count * neighbour_ids.shape[1]
    capacity = per_reader // 2
    db_count = database.shape[0]
    ret_len = database.shape[1]
    col_count = database.shape[2]
    head_cols = w_query.shape[1]
    heads_local = head_cols // HD
    group_len = tok_rows // group_count
    skipped = (group_len - 1) // 16 * 16
    own_head = (
        jnp.arange(head_cols)[None, :] // HD == jnp.arange(heads_local)[:, None]
    )
    last_hidden = lax.all_gather(hidden[tok_rows - 16 :], "tensor", axis=1, tiled=True)
    last_query = jnp.dot(last_hidden, w_query, preferred_element_type=jnp.float32)
    last_query = jnp.where(own_head, last_query[15:].astype(jnp.bfloat16), 0)
    lifted = lax.dot_general(
        last_query, w_key, (((1,), (1,)), ((), ())), preferred_element_type=jnp.float32
    ).astype(jnp.bfloat16)
    lifted = lax.all_gather(lifted, "tensor", axis=0, tiled=True)
    late_hidden, lifted = lax.optimization_barrier((hidden[skipped:], lifted))
    all_hidden = lax.all_gather(late_hidden, "tensor", axis=1, tiled=True)
    block_ids = neighbour_ids.reshape(per_reader)
    owners = block_ids // db_count
    earlier = jnp.arange(per_reader)[:, None] > jnp.arange(per_reader)[None, :]
    slot_rank = jnp.sum(((owners[:, None] == owners[None, :]) & earlier).astype(jnp.int32), 1)
    slot_range = jnp.arange(capacity, dtype=jnp.int32)
    local_index = block_ids % db_count
    owner_range = jnp.arange(dp_count, dtype=jnp.int32)
    slot_hit = (owners[:, None, None] == owner_range[None, :, None]) & (
        slot_rank[:, None, None] == slot_range[None, None, :]
    )
    request_table = jnp.sum(slot_hit.astype(jnp.int32) * local_index[:, None, None], 0)
    requested = lax.all_to_all(request_table, "dp", split_axis=0, concat_axis=0, tiled=True)
    outgoing = jnp.take(database, requested.reshape(-1), axis=0, mode="clip").reshape(
        dp_count, capacity, ret_len, col_count
    )
    arrived = lax.all_to_all(outgoing, "dp", split_axis=0, concat_axis=0, tiled=True)
    neighbour_rows = jnp.take(
        arrived.reshape(dp_count * capacity, ret_len, col_count),
        owners * capacity + slot_rank,
        axis=0,
        mode="clip",
    )
    neighbour_rows = neighbour_rows.reshape(per_reader * ret_len, col_count)
    full_rows = (group_count - 1) * (per_reader // group_count) * ret_len
    last_rows = neighbour_rows[full_rows:]
    place = lax.axis_index("tensor")
    lifted = lax.dynamic_slice_in_dim(lifted, place * col_count, col_count, 1)
    last_part = lax.dot_general(
        lifted, last_rows, (((1,), (1,)), ((), ())), preferred_element_type=jnp.float32
    )
    first_rows, last_part = lax.optimization_barrier((neighbour_rows[:full_rows], last_part))
    last_scores = lax.psum(last_part, "tensor")
    key_rows, value_rows = neighbour_keys(first_rows, w_key, w_value, group_count - 1)
    key_rows, last_scores = lax.optimization_barrier((key_rows, last_scores))
    last_soft = softmax(last_scores / jnp.sqrt(jnp.float32(HD)))
    last_mix = jnp.dot(
        last_soft, last_rows, preferred_element_type=jnp.float32
    ).astype(jnp.bfloat16)
    last_mix = lax.all_gather(last_mix, "tensor", axis=1, tiled=True)
    key_rows, all_hidden = lax.optimization_barrier((key_rows, all_hidden))
    query_rows = jnp.dot(
        all_hidden, w_query, preferred_element_type=jnp.float32
    ).astype(jnp.bfloat16)
    lead = group_len - 1 - skipped
    blended = attend(query_rows[lead:-1], key_rows, value_rows, heads_local, group_len)
    last_mix = lax.dynamic_slice_in_dim(last_mix, place * heads_local, heads_local, 0)
    last_context = jnp.dot(last_mix, w_value, preferred_element_type=jnp.float32)
    last_context = jnp.sum(jnp.where(own_head, last_context, 0), 0, keepdims=True)
    context = jnp.concatenate(
        [
            jnp.zeros((lead, head_cols), jnp.bfloat16),
            blended,
            last_context.astype(jnp.bfloat16),
        ],
        0,
    )
    mixed = project_out(context, w_out)
    return jnp.concatenate([jnp.zeros((skipped, mixed.shape[1]), mixed.dtype), mixed], 0)


def solution(mesh):
    placed = (
        P("dp", "tensor"),
        P("dp", None),
        P("dp", None, "tensor"),
        P(None, "tensor"),
        P(None, "tensor"),
        P(None, "tensor"),
        P("tensor", None),
    )
    return jax.shard_map(
        shards, mesh=mesh, in_specs=placed, out_specs=P("dp", "tensor"), check_vma=False
    )
```

```python
import functools

import jax
import jax.numpy as jnp
from jax import lax
from jax.experimental import pallas as pl
from jax.experimental.pallas import tpu as pltpu
from jax.sharding import PartitionSpec as P

MESH = pl.DeviceIdType.MESH

HD = 128


def attend(query_rows, key_rows, value_rows, heads_count, group_len):
    width = query_rows.shape[1]
    groups = query_rows.shape[0] // group_len
    head_size = width // heads_count
    shifted = query_rows.reshape(groups, group_len, heads_count, head_size)
    key_block = key_rows.reshape(groups, -1, heads_count, head_size)
    value_block = value_rows.reshape(groups, -1, heads_count, head_size)
    scores = jnp.einsum(
        "cqhd,ckhd->chqk", shifted, key_block, preferred_element_type=jnp.float32
    ) / jnp.sqrt(jnp.float32(head_size))
    soft = softmax(scores)
    blended = jnp.einsum(
        "chqk,ckhd->cqhd", soft, value_block, preferred_element_type=jnp.float32
    ).astype(jnp.bfloat16)
    return blended.reshape(groups * group_len, width)


def softmax(scores):
    top_score = jnp.max(scores, axis=-1, keepdims=True)
    weights_raw = jnp.exp(scores - top_score)
    return (weights_raw / jnp.sum(weights_raw, axis=-1, keepdims=True)).astype(jnp.bfloat16)


def plane(tensor_count):
    nz = 4 if tensor_count % 4 == 0 else 1
    return nz, tensor_count // nz


def gather_project(
    nz, ny, x_ref, wk_ref, wv_ref, k_ref, v_ref,
    held, wk_held, wv_held, total, send_sem, recv_sem, local_sem,
):
    chunks, rows, feats = x_ref.shape
    cols = wk_ref.shape[1]
    me = lax.axis_index("tensor")
    z, y = me // ny, me % ny
    up, down, right, left = z + 1 < nz, z >= 1, y + 1 < ny, y >= 1

    own_copy = pltpu.make_async_copy(x_ref, held.at[me], local_sem.at[0])
    own_copy.start()
    wk_copy = pltpu.make_async_copy(wk_ref, wk_held, local_sem.at[1])
    wk_copy.start()
    wv_copy = pltpu.make_async_copy(wv_ref, wv_held, local_sem.at[2])
    wv_copy.start()

    barrier = pltpu.get_barrier_semaphore()
    sides = ((up, ny), (down, -ny), (right, 1), (left, -1))
    for there, step in sides:
        @pl.when(there)
        def _():
            pl.semaphore_signal(
                barrier, inc=1, device_id={"tensor": me + step}, device_id_type=MESH
            )
    pl.semaphore_wait(barrier, sum(there.astype(jnp.int32) for there, _ in sides))

    def move(side, shard, c):
        return pltpu.make_async_remote_copy(
            src_ref=held.at[shard, c],
            dst_ref=held.at[shard, c],
            send_sem=send_sem.at[side, shard, c],
            recv_sem=recv_sem.at[shard, c],
            device_id={"tensor": me + sides[side][1]},
            device_id_type=MESH,
        )

    def send(side, shard, c, cond):
        @pl.when(cond & sides[side][0])
        def _():
            move(side, shard, c).start()

    def landed(shard, c):
        move(0, shard, c).wait_recv()

    total[...] = jnp.zeros_like(total)
    own_copy.wait()

    def column(e):
        step = (e + 1) // 2
        above = e % 2 == 0
        zc = jnp.where(above, z + step, z - step)
        return zc, above, step, (zc >= 0) & (zc < nz) & (e >= 0) & (e < 2 * nz - 1)

    def project(shard):
        w_rows = pl.ds(pl.multiple_of(shard * feats, feats), feats)

        @pl.loop(0, chunks)
        def _(c):
            block = held[shard, c]
            total[c, :, :cols] += jnp.dot(
                block, wk_held[w_rows, :], preferred_element_type=jnp.float32
            )
            total[c, :, cols:] += jnp.dot(
                block, wv_held[w_rows, :], preferred_element_type=jnp.float32
            )

    def event(e, carry):
        zc, above, step, valid = column(e)

        @pl.when(valid)
        def _():
            shard = zc * ny + y
            for c in range(chunks):
                @pl.when(step > 0)
                def _():
                    landed(shard, c)

                send(0, shard, c, (step == 0) | jnp.logical_not(above))
                send(1, shard, c, above)
                send(2, shard, c, True)
                send(3, shard, c, True)

            @pl.when(step == 0)
            def _():
                wk_copy.wait()
                wv_copy.wait()

            project(shard)

        zl, _, _, late = column(e - 2)
        for m in range(1, ny):
            for sign in (-1, 1):
                yc = y + sign * m

                @pl.when(late & (yc >= 0) & (yc < ny))
                def _():
                    shard = zl * ny + yc
                    for c in range(chunks):
                        landed(shard, c)
                        if ny > 2:
                            send(2 if sign < 0 else 3, shard, c, True)
                    project(shard)
        return carry

    lax.fori_loop(0, 2 * nz + 1, event, 0)

    k_ref[...] = total[:, :, :cols].astype(jnp.bfloat16)
    v_ref[...] = total[:, :, cols:].astype(jnp.bfloat16)

    def finish(shard, carry):
        zs, ys = shard // ny, shard % ny
        mine = ys == y
        went = (mine & (zs <= z), mine & (zs >= z), ys <= y, ys >= y)
        for side in range(4):
            @pl.when(went[side] & sides[side][0])
            def _():
                for c in range(chunks):
                    move(side, shard, c).wait_send()
        return carry

    lax.fori_loop(0, nz * ny, finish, 0)


def neighbour_keys(rows, w_key, w_value, chunks):
    tensor_count = lax.axis_size("tensor")
    nz, ny = plane(tensor_count)
    row_count, feats = rows.shape
    cols = w_key.shape[1]
    per = row_count // chunks
    out = jax.ShapeDtypeStruct((chunks, per, cols), jnp.bfloat16)
    keys, values = pl.pallas_call(
        functools.partial(gather_project, nz, ny),
        out_shape=(out, out),
        in_specs=[pl.BlockSpec(memory_space=pl.ANY)] * 3,
        out_specs=(pl.BlockSpec(memory_space=pltpu.VMEM),) * 2,
        scratch_shapes=[
            pltpu.VMEM((tensor_count, chunks, per, feats), jnp.bfloat16),
            pltpu.VMEM(w_key.shape, jnp.bfloat16),
            pltpu.VMEM(w_value.shape, jnp.bfloat16),
            pltpu.VMEM((chunks, per, 2 * cols), jnp.float32),
            pltpu.SemaphoreType.DMA((4, tensor_count, chunks)),
            pltpu.SemaphoreType.DMA((tensor_count, chunks)),
            pltpu.SemaphoreType.DMA((3,)),
        ],
        compiler_params=pltpu.CompilerParams(
            collective_id=0, has_side_effects=True, vmem_limit_bytes=56 * 2**20
        ),
        cost_estimate=pl.CostEstimate(
            flops=4 * row_count * feats * tensor_count * cols,
            bytes_accessed=4 * w_key.size,
            transcendentals=0,
        ),
    )(rows.reshape(chunks, per, feats), w_key, w_value)
    return keys.reshape(row_count, cols), values.reshape(row_count, cols)


def project_scatter(
    nz, ny, ctx_ref, w_ref, out_ref, w_held, outgoing, from_y, from_z,
    total, send_sem, recv_y, recv_z, local_sem,
):
    feats = out_ref.shape[1]
    count = nz * ny
    me = lax.axis_index("tensor")
    z, y = me // ny, me % ny
    up, down, right, left = z + 1 < nz, z >= 1, y + 1 < ny, y >= 1
    sides = ((up, ny), (down, -ny), (right, 1), (left, -1))

    def load(dest):
        columns = pl.ds(pl.multiple_of(dest * feats, feats), feats)
        return pltpu.make_async_copy(
            w_ref.at[:, columns], w_held.at[dest], local_sem.at[dest]
        )

    def column(e):
        step = (e + 1) // 2
        above = e % 2 == 0
        zc = jnp.where(above, z + step, z - step)
        return zc, above, (zc >= 0) & (zc < nz) & (e >= 0) & (e < 2 * nz - 1)

    def fetch(i, carry):
        zc, _, valid = column(2 * nz - 2 - i)

        @pl.when(valid)
        def _():
            for off in range(1, ny + 1):
                load(zc * ny + (y + off) % ny).start()
        return carry

    lax.fori_loop(0, 2 * nz - 1, fetch, 0)

    barrier = pltpu.get_barrier_semaphore()
    for there, step in sides:
        @pl.when(there)
        def _():
            pl.semaphore_signal(
                barrier, inc=1, device_id={"tensor": me + step}, device_id_type=MESH
            )
    pl.semaphore_wait(barrier, sum(there.astype(jnp.int32) for there, _ in sides))

    def along_y(side, dest):
        return pltpu.make_async_remote_copy(
            src_ref=outgoing.at[dest],
            dst_ref=from_y.at[side, dest],
            send_sem=send_sem.at[dest],
            recv_sem=recv_y.at[side, dest],
            device_id={"tensor": me + (1 if side == 0 else -1)},
            device_id_type=MESH,
        )

    def along_z(side, dest):
        return pltpu.make_async_remote_copy(
            src_ref=outgoing.at[dest],
            dst_ref=from_z.at[side, dest // ny],
            send_sem=send_sem.at[dest],
            recv_sem=recv_z.at[side, dest // ny],
            device_id={"tensor": me + (ny if side == 0 else -ny)},
            device_id_type=MESH,
        )

    def own_share(dest):
        load(dest).wait()
        return jnp.dot(ctx_ref[...], w_held[dest], preferred_element_type=jnp.float32)

    def event(i, carry):
        zc, _, valid = column(2 * nz - 2 - i)
        for m in range(ny - 1, 0, -1):
            for side in (0, 1):
                yc = y + m if side == 0 else y - m

                @pl.when(valid & (yc >= 0) & (yc < ny))
                def _():
                    dest = zc * ny + yc
                    share = own_share(dest)
                    outgoing[dest] = share.astype(jnp.bfloat16)
                    if ny > 2:
                        @pl.when(left if side == 0 else right)
                        def _():
                            along_y(side, dest).wait_recv()
                            outgoing[dest] = (
                                share + from_y[side, dest].astype(jnp.float32)
                            ).astype(jnp.bfloat16)
                    along_y(side, dest).start()

        zl, above, late = column(2 * nz - 2 - i + 2)

        @pl.when(late)
        def _():
            dest = zl * ny + y
            share = own_share(dest)
            total[...] = share
            for side, there in ((0, left), (1, right)):
                @pl.when(there)
                def _():
                    along_y(side, dest).wait_recv()
                    total[...] += from_y[side, dest].astype(jnp.float32)
            for side, there in ((0, down & (zl >= z)), (1, up & (zl <= z))):
                @pl.when(there)
                def _():
                    along_z(side, dest).wait_recv()
                    total[...] += from_z[side, zl].astype(jnp.float32)

            @pl.when(zl == z)
            def _():
                out_ref[...] = total[...].astype(jnp.bfloat16)

            @pl.when(zl != z)
            def _():
                outgoing[dest] = total[...].astype(jnp.bfloat16)

            @pl.when(zl > z)
            def _():
                along_z(0, dest).start()

            @pl.when(zl < z)
            def _():
                along_z(1, dest).start()
        return carry

    lax.fori_loop(0, 2 * nz + 1, event, 0)

    def finish(dest, carry):
        @pl.when(dest != me)
        def _():
            along_y(0, dest).wait_send()
        return carry

    lax.fori_loop(0, count, finish, 0)


def project_out(context, w_out):
    tensor_count = lax.axis_size("tensor")
    nz, ny = plane(tensor_count)
    rows, depth = context.shape
    feats = w_out.shape[1] // tensor_count
    return pl.pallas_call(
        functools.partial(project_scatter, nz, ny),
        out_shape=jax.ShapeDtypeStruct((rows, feats), jnp.bfloat16),
        in_specs=[
            pl.BlockSpec(memory_space=pltpu.VMEM),
            pl.BlockSpec(memory_space=pl.ANY),
        ],
        out_specs=pl.BlockSpec(memory_space=pltpu.VMEM),
        scratch_shapes=[
            pltpu.VMEM((tensor_count, depth, feats), jnp.bfloat16),
            pltpu.VMEM((tensor_count, rows, feats), jnp.bfloat16),
            pltpu.VMEM((2, tensor_count, rows, feats), jnp.bfloat16),
            pltpu.VMEM((2, nz, rows, feats), jnp.bfloat16),
            pltpu.VMEM((rows, feats), jnp.float32),
            pltpu.SemaphoreType.DMA((tensor_count,)),
            pltpu.SemaphoreType.DMA((2, tensor_count)),
            pltpu.SemaphoreType.DMA((2, nz)),
            pltpu.SemaphoreType.DMA((tensor_count,)),
        ],
        compiler_params=pltpu.CompilerParams(
            collective_id=1, has_side_effects=True, vmem_limit_bytes=48 * 2**20
        ),
        cost_estimate=pl.CostEstimate(
            flops=2 * rows * w_out.size, bytes_accessed=2 * w_out.size, transcendentals=0
        ),
    )(context, w_out)


def shards(hidden, neighbour_ids, database, w_query, w_key, w_value, w_out):
    dp_count = lax.axis_size("dp")
    tok_rows = hidden.shape[0]
    group_count = neighbour_ids.shape[0]
    per_reader = group_count * neighbour_ids.shape[1]
    capacity = per_reader // 2
    db_count = database.shape[0]
    ret_len = database.shape[1]
    col_count = database.shape[2]
    head_cols = w_query.shape[1]
    heads_local = head_cols // HD
    group_len = tok_rows // group_count
    skipped = (group_len - 1) // 16 * 16
    own_head = (
        jnp.arange(head_cols)[None, :] // HD == jnp.arange(heads_local)[:, None]
    )
    all_hidden = lax.all_gather(hidden[skipped:], "tensor", axis=1, tiled=True)
    query_rows = jnp.dot(
        all_hidden, w_query, preferred_element_type=jnp.float32
    ).astype(jnp.bfloat16)
    last_query = jnp.where(own_head, query_rows[-1:], 0)
    lifted = lax.dot_general(
        last_query, w_key, (((1,), (1,)), ((), ())), preferred_element_type=jnp.float32
    ).astype(jnp.bfloat16)
    lifted = lax.all_to_all(lifted, "tensor", split_axis=1, concat_axis=0, tiled=True)
    block_ids = neighbour_ids.reshape(per_reader)
    owners = block_ids // db_count
    earlier = jnp.arange(per_reader)[:, None] > jnp.arange(per_reader)[None, :]
    slot_rank = jnp.sum(((owners[:, None] == owners[None, :]) & earlier).astype(jnp.int32), 1)
    slot_range = jnp.arange(capacity, dtype=jnp.int32)
    local_index = block_ids % db_count
    owner_range = jnp.arange(dp_count, dtype=jnp.int32)
    slot_hit = (owners[:, None, None] == owner_range[None, :, None]) & (
        slot_rank[:, None, None] == slot_range[None, None, :]
    )
    request_table = jnp.sum(slot_hit.astype(jnp.int32) * local_index[:, None, None], 0)
    requested = lax.all_to_all(request_table, "dp", split_axis=0, concat_axis=0, tiled=True)
    outgoing = jnp.take(database, requested.reshape(-1), axis=0, mode="clip").reshape(
        dp_count, capacity, ret_len, col_count
    )
    arrived = lax.all_to_all(outgoing, "dp", split_axis=0, concat_axis=0, tiled=True)
    neighbour_rows = jnp.take(
        arrived.reshape(dp_count * capacity, ret_len, col_count),
        owners * capacity + slot_rank,
        axis=0,
        mode="clip",
    )
    neighbour_rows = neighbour_rows.reshape(per_reader * ret_len, col_count)
    full_rows = (group_count - 1) * (per_reader // group_count) * ret_len
    last_rows = neighbour_rows[full_rows:]
    last_part = lax.dot_general(
        lifted, last_rows, (((1,), (1,)), ((), ())), preferred_element_type=jnp.float32
    )
    first_rows, last_part = lax.optimization_barrier((neighbour_rows[:full_rows], last_part))
    last_part = jnp.broadcast_to(last_part, (lax.axis_size("tensor"),) + last_part.shape)
    last_scores = jnp.sum(
        lax.all_to_all(last_part, "tensor", split_axis=0, concat_axis=0, tiled=True), 0
    )
    key_rows, value_rows = neighbour_keys(first_rows, w_key, w_value, group_count - 1)
    key_rows, last_scores = lax.optimization_barrier((key_rows, last_scores))
    last_soft = softmax(last_scores / jnp.sqrt(jnp.float32(HD)))
    last_mix = jnp.dot(
        last_soft, last_rows, preferred_element_type=jnp.float32
    ).astype(jnp.bfloat16)
    last_mix = lax.all_to_all(last_mix, "tensor", split_axis=0, concat_axis=1, tiled=True)
    lead = group_len - 1 - skipped
    blended = attend(query_rows[lead:-1], key_rows, value_rows, heads_local, group_len)
    last_context = jnp.dot(last_mix, w_value, preferred_element_type=jnp.float32)
    last_context = jnp.sum(jnp.where(own_head, last_context, 0), 0, keepdims=True)
    context = jnp.concatenate(
        [
            jnp.zeros((lead, head_cols), jnp.bfloat16),
            blended,
            last_context.astype(jnp.bfloat16),
        ],
        0,
    )
    mixed = project_out(context, w_out)
    return jnp.concatenate([jnp.zeros((skipped, mixed.shape[1]), mixed.dtype), mixed], 0)


def solution(mesh):
    placed = (
        P("dp", "tensor"),
        P("dp", None),
        P("dp", None, "tensor"),
        P(None, "tensor"),
        P(None, "tensor"),
        P(None, "tensor"),
        P("tensor", None),
    )
    return jax.shard_map(
        shards, mesh=mesh, in_specs=placed, out_specs=P("dp", "tensor"), check_vma=False
    )
```
